128 devices in a mesh: seg: 16 (over y_lo, x, core), chan: 8 (over y_hi, z).
Axes of the slice: x: 4, y: 4 (y_hi: 2, y_lo: 2; y = y_hi * 2 + y_lo), z: 4, core: 2. Of those that a mesh axis runs over, the one named last changes fastest.
Arguments:
- signal: bfloat16 [256, 256, 2048], P('seg', 'chan'), may hold values from -6 to 6
- latent_factor: float32 [512, 256], replicated, may hold values from -0.375 to 0.375
Outputs:
- smoothed: float32 [512, 256, 2, 256], P(None, ('seg', 'chan'))
The draws below stay inside these ranges and needn't reach their ends.
All inputs are finite; a program needn't handle non-finite values.
Results may differ from the reference program's by a relative error of at most 0.02.
Values may be sent and summed in bfloat16 or wider, within the bound.
A program may use at most 128 MiB of HBM per device.

```python
import math
import jax
import jax.numpy as jnp
from jax import lax

C = 256
L = 2048
NF = 512
R = 256
S_DEV = 16
SEGS = 256
N_SEG = 16


def block_scale(own_key, extent, pieces, smallest, top_value):
    factor_of = 1.0
    for axis_at, parts in pieces:
        heights = jax.random.uniform(jax.random.fold_in(jax.random.fold_in(own_key, 6), axis_at), (parts,), jnp.float32, smallest / len(pieces), top_value / len(pieces))
        factor_of = factor_of * jnp.repeat(jnp.exp(heights), extent[axis_at] // parts).reshape((-1,) + (1,) * (len(extent) - 1 - axis_at))
    return factor_of


def scatter_about(rng, shape, spread, most, shards=(), kind=jnp.bfloat16):
    values = spread * jax.random.normal(rng, shape, jnp.float32)
    if shards:
        values = values * block_scale(rng, shape, shards, -0.22, 0.18)
    return jnp.clip(values, -most, most).astype(kind)


def setup_inputs(seed: int = 0) -> dict:
    key_list = jax.random.split(jax.random.key(seed), 3)
    signal = scatter_about(key_list[0], (SEGS, C, L), 1.0, 6.0, ((0, 16), (1, 8)))
    latent_factor = scatter_about(key_list[1], (NF, R), R ** -0.5, 0.375, (), jnp.float32)
    return {"signal": signal, "latent_factor": latent_factor}


def dft_table(length, bins):
    times = jnp.arange(length, dtype=jnp.int32)
    freqs = jnp.arange(bins, dtype=jnp.int32)
    phase = times[:, None] * freqs[None, :] % length
    theta = 2.0 * math.pi * phase.astype(jnp.float32) / length
    window = 0.5 - 0.5 * jnp.cos(2.0 * math.pi * times.astype(jnp.float32) / length)
    weight = window / jnp.sqrt(jnp.float32(3.0 * length / 8.0))
    cos_part = weight[:, None] * jnp.cos(theta)
    sin_part = -weight[:, None] * jnp.sin(theta)
    return jnp.stack([cos_part, sin_part], axis=1).astype(jnp.bfloat16)

def cross_terms(spectra, segs):
    real_part = spectra[:, :, 0, :]
    imag_part = spectra[:, :, 1, :]
    high = lax.Precision.HIGHEST
    same = jnp.einsum('fsc,fsd->fcd', real_part, real_part, precision=high) + jnp.einsum('fsc,fsd->fcd', imag_part, imag_part, precision=high)
    twist = jnp.einsum('fsc,fsd->fcd', real_part, imag_part, precision=high) - jnp.einsum('fsc,fsd->fcd', imag_part, real_part, precision=high)
    return jnp.stack([same, twist], axis=2) * (1.0 / segs)

def reference(signal, latent_factor):
    table = dft_table(L, NF).astype(jnp.float32)
    groups = signal.reshape(N_SEG, S_DEV, C, L)

    def add_group(total, block):
        spectra = jnp.einsum('scl,lkf->fskc', block.astype(jnp.float32), table, precision=lax.Precision.HIGHEST)
        spectra = lax.optimization_barrier(spectra.astype(jnp.bfloat16)).astype(jnp.float32)
        term = cross_terms(spectra, SEGS)
        term = lax.optimization_barrier(term.astype(jnp.bfloat16)).astype(jnp.float32)
        return (total + term, None)
    cross, _ = lax.scan(add_group, jnp.zeros((NF, C, 2, C), jnp.float32), groups)
    latent = jnp.einsum('fr,fckd->rckd', latent_factor, cross, precision=lax.Precision.HIGHEST)
    return jnp.einsum('fr,rckd->fckd', latent_factor, latent, precision=lax.Precision.HIGHEST)
```

```python
import functools

import jax
import jax.numpy as jnp
import ml_dtypes
import numpy as np
from jax import lax
from jax.experimental import pallas as pl
from jax.experimental.pallas import tpu as pltpu
from jax.sharding import PartitionSpec as P

MESH = pl.DeviceIdType.MESH
HALVES = 2
NT = (((1,), (1,)), ((), ()))


def dft_rows(length, bins, devices):
    per_half = bins // devices // HALVES
    half, owner, at = np.meshgrid(
        np.arange(HALVES), np.arange(devices), np.arange(per_half), indexing="ij"
    )
    freqs = ((half * per_half + at) * devices + owner).reshape(-1)
    times = np.arange(length)
    theta = 2.0 * np.pi * (freqs[:, None] * times[None, :] % length) / length
    weight = (0.5 - 0.5 * np.cos(2.0 * np.pi * times / length)) / np.sqrt(3.0 * length / 8.0)
    rows = np.stack([weight * np.cos(theta), -weight * np.sin(theta)], axis=1)
    return rows.reshape(-1, length).astype(np.float32).astype(ml_dtypes.bfloat16)


def kernel(
    n_seg, n_chan, segs,
    sig_hbm, tab_hbm, lat_hbm, out_ref,
    sig, tab, lat, send1, recv1, send2, recv2, z, scr, m_hi, m_lo, acc,
    in_sem, send_sem, recv_sem,
):
    n = n_seg * n_chan
    seg, chan = lax.axis_index("seg"), lax.axis_index("chan")
    me = seg * n_chan + chan
    slot = chan * n_seg + seg
    half_rows = tab.shape[0] // HALVES
    bins = m_hi.shape[0]

    sig_in = pltpu.make_async_copy(sig_hbm, sig, in_sem.at[0])
    sig_in.start()
    tab_in = []
    for h in range(HALVES):
        rows = pl.ds(h * half_rows, half_rows)
        tab_in.append(pltpu.make_async_copy(tab_hbm.at[rows], tab.at[rows], in_sem.at[1 + h]))
        tab_in[-1].start()
    lat_in = pltpu.make_async_copy(lat_hbm, lat, in_sem.at[3])
    lat_in.start()

    def coords(d):
        return lax.div(d, n_chan), lax.rem(d, n_chan)

    barrier = pltpu.get_barrier_semaphore()

    def greet(s, carry):
        pl.semaphore_signal(
            barrier, inc=1, device_id=coords(lax.rem(me + s, n)), device_id_type=MESH
        )
        return carry

    lax.fori_loop(1, n, greet, 0)

    def transform(h):
        step = 128
        low = lax.broadcasted_iota(jnp.int32, (step, 128), 0) % 8 < 4

        def block(i, carry):
            rows = pl.ds(pl.multiple_of(h * half_rows + i * step, step), step)
            y = lax.dot_general(tab[rows, :], sig[...], NT, preferred_element_type=jnp.float32)
            v = [y[:, q * 128 : (q + 1) * 128] for q in range(4)]
            up = [pltpu.roll(a, 4, 0) for a in v]
            even = [jnp.where(low, v[q], up[q + 1]) for q in (0, 2)]
            down = [pltpu.roll(a, step - 4, 0) for a in v]
            odd = [jnp.where(low, down[q], v[q + 1]) for q in (0, 2)]
            pairs = step // 8
            both = [
                jnp.concatenate([a.reshape(pairs, 1, 8, 128) for a in part], axis=2)
                for part in (even, odd)
            ]
            block = jnp.concatenate(both, axis=1).reshape(2 * pairs, 16, 128)
            send1[h, pl.ds(i * 2 * pairs, 2 * pairs)] = block.astype(jnp.bfloat16)
            return carry

        lax.fori_loop(0, half_rows // step, block, 0)

    def send(k, src, dst, at):
        def one(s, carry):
            d = lax.rem(me + s, n)
            pltpu.make_async_remote_copy(
                src_ref=src.at[d], dst_ref=dst.at[at], send_sem=send_sem.at[k],
                recv_sem=recv_sem.at[k], device_id=coords(d), device_id_type=MESH,
            ).start()
            return carry

        lax.fori_loop(1, n, one, 0)
        pltpu.make_async_copy(src.at[me], dst.at[at], recv_sem.at[k]).start()

    def arrived(k, src, dst):
        pltpu.make_async_copy(src, dst, recv_sem.at[k]).wait()

    def cross(h):
        width = n_seg * 16
        for j in range(n_chan):
            t = recv1[h, j * n_seg : (j + 1) * n_seg].reshape(width, 128).T
            for s in range(4):
                z[j * 32 : (j + 1) * 32, s * width : (s + 1) * width] = t[s * 32 : (s + 1) * 32]
        zf = z[...].astype(jnp.float32)
        lane = lax.broadcasted_iota(jnp.int32, zf.shape, 1) % 4
        last = zf.shape[1] - 1
        y = jnp.where(lane % 2 == 0, pltpu.roll(zf, last, 1), -pltpu.roll(zf, 1, 1))
        for b in range(2):
            own = lane // 2 == b
            for k, part in enumerate((zf, y)):
                right = jnp.where(own, part, 0.0).astype(jnp.bfloat16)
                c = lax.dot_general(z[...], right, NT, preferred_element_type=jnp.float32)
                for dh in range(2):
                    at = b * 4 + k * 2 + dh
                    scr[pl.ds(at, c.shape[0], stride=8), :] = c[:, dh * 128 : (dh + 1) * 128]
        send2[h] = scr[...].reshape(n, 16, 128).astype(jnp.bfloat16)

    def smooth(h):
        scr[...] = recv2[h].reshape(n * 16, 128).astype(jnp.float32)
        left = pl.ds(h * 2 * n, 2 * n)
        for c in range(2):
            for dh in range(2):
                for k in range(2):
                    at = c * 4 + dh * 2 + k
                    x = jnp.concatenate(
                        [
                            scr[pl.ds(c * 8 + b * 4 + k * 2 + dh, n, stride=16), :]
                            for b in range(2)
                        ],
                        axis=0,
                    ).astype(jnp.bfloat16)
                    r = jnp.dot(m_hi[:, left], x, preferred_element_type=jnp.float32)
                    r = r + jnp.dot(m_lo[:, left], x, preferred_element_type=jnp.float32)
                    if h == 0:
                        acc[at] = r
                    else:
                        out_ref[pl.ds(at, bins, stride=8), :] = r + acc[at]

    sig_in.wait()
    tab_in[0].wait()
    transform(0)
    pl.semaphore_wait(barrier, n - 1)
    send(0, send1.at[0], recv1.at[0], slot)
    tab_in[1].wait()
    transform(1)
    send(1, send1.at[1], recv1.at[1], slot)
    lat_in.wait()
    m = lax.dot_general(
        lat[...], lat[...], NT, preferred_element_type=jnp.float32, precision=lax.Precision.HIGHEST
    ) * (1.0 / segs)
    m_hi[...] = m.astype(jnp.bfloat16)
    m_lo[...] = (m - m_hi[...].astype(jnp.float32)).astype(jnp.bfloat16)
    for h in range(HALVES):
        arrived(h, send1.at[h], recv1.at[h])
        cross(h)
        send(2 + h, send2.at[h], recv2.at[h], me)
    for h in range(HALVES):
        arrived(2 + h, send2.at[h], recv2.at[h])
        smooth(h)
    for k in range(2 * HALVES):
        src = (send1, send2)[k // HALVES].at[k % HALVES, pl.ds(0, n - 1)]
        pltpu.make_async_copy(src, src, send_sem.at[k]).wait()


def per_device(signal, latent_factor):
    seg_count, chan_local, length = signal.shape
    bins, rank = latent_factor.shape
    n_seg = lax.axis_size("seg")
    n_chan = lax.axis_size("chan")
    n = n_seg * n_chan
    channels = chan_local * n_chan
    table = jnp.asarray(dft_rows(length, bins, n))
    bf16, f32 = jnp.bfloat16, jnp.float32
    out = pl.pallas_call(
        functools.partial(kernel, n_seg, n_chan, seg_count * n_seg),
        out_shape=jax.ShapeDtypeStruct((bins * 8, 128), f32),
        in_specs=[pl.BlockSpec(memory_space=pl.ANY)] * 3,
        out_specs=pl.BlockSpec(memory_space=pltpu.VMEM),
        scratch_shapes=[
            pltpu.VMEM((seg_count * chan_local, length), bf16),
            pltpu.VMEM(table.shape, bf16),
            pltpu.VMEM((bins, rank), f32),
            pltpu.VMEM((HALVES, n, 16, 128), bf16),
            pltpu.VMEM((HALVES, n, 16, 128), bf16),
            pltpu.VMEM((HALVES, n, 16, 128), bf16),
            pltpu.VMEM((HALVES, n, 16, 128), bf16),
            pltpu.VMEM((channels, 64 * n_seg), bf16),
            pltpu.VMEM((n * 16, 128), f32),
            pltpu.VMEM((bins, bins), bf16),
            pltpu.VMEM((bins, bins), bf16),
            pltpu.VMEM((8, bins, 128), f32),
            pltpu.SemaphoreType.DMA((4,)),
            pltpu.SemaphoreType.DMA((2 * HALVES,)),
            pltpu.SemaphoreType.DMA((2 * HALVES,)),
        ],
        compiler_params=pltpu.CompilerParams(
            collective_id=0, has_side_effects=True, vmem_limit_bytes=48 * 2**20
        ),
    )(signal.reshape(seg_count * chan_local, length), table, latent_factor)
    out = out.reshape(bins, 2, 2, 2, 128).transpose(0, 1, 3, 2, 4)
    return out.reshape(bins, channels // n, 2, channels)


def solution(mesh):
    in_specs = (P("seg", "chan", None), P())
    out_specs = P(None, ("seg", "chan"), None, None)
    return jax.shard_map(
        per_device, mesh=mesh, in_specs=in_specs, out_specs=out_specs, check_vma=False
    )
```

```python
import functools
import random

import jax
import jax.numpy as jnp
import ml_dtypes
import numpy as np
from jax import lax
from jax.experimental import pallas as pl
from jax.experimental.pallas import tpu as pltpu
from jax.sharding import PartitionSpec as P

MESH = pl.DeviceIdType.MESH
HALVES = 2
SIDE = 4
NT = (((1,), (1,)), ((), ()))


def far_first():
    steps = [(z, y, x, c) for x in range(SIDE) for y in range(SIDE) for z in range(SIDE) for c in range(2)][1:]
    random.Random(1).shuffle(steps)
    return sorted(steps, key=lambda step: -sum(min(v, SIDE - v) for v in step[:3]))


def dft_rows(length, bins, devices):
    per_half = bins // devices // HALVES
    half, owner, at = np.meshgrid(
        np.arange(HALVES), np.arange(devices), np.arange(per_half), indexing="ij"
    )
    freqs = ((half * per_half + at) * devices + owner).reshape(-1)
    times = np.arange(length)
    theta = 2.0 * np.pi * (freqs[:, None] * times[None, :] % length) / length
    weight = (0.5 - 0.5 * np.cos(2.0 * np.pi * times / length)) / np.sqrt(3.0 * length / 8.0)
    rows = np.stack([weight * np.cos(theta), -weight * np.sin(theta)], axis=1)
    return rows.reshape(-1, length).astype(np.float32).astype(ml_dtypes.bfloat16)


def kernel(
    n_seg, n_chan, segs,
    sig_hbm, tab_hbm, lat_hbm, out_ref,
    sig, tab, lat, send1, recv1, send2, recv2, z, scr, m_hi, m_lo, acc,
    in_sem, send_sem, recv_sem,
):
    n = n_seg * n_chan
    seg, chan = lax.axis_index("seg"), lax.axis_index("chan")
    me = seg * n_chan + chan
    slot = chan * n_seg + seg
    half_rows = tab.shape[0] // HALVES
    bins = m_hi.shape[0]

    sig_in = pltpu.make_async_copy(sig_hbm, sig, in_sem.at[0])
    sig_in.start()
    tab_in = []
    for h in range(HALVES):
        rows = pl.ds(h * half_rows, half_rows)
        tab_in.append(pltpu.make_async_copy(tab_hbm.at[rows], tab.at[rows], in_sem.at[1 + h]))
        tab_in[-1].start()
    lat_in = pltpu.make_async_copy(lat_hbm, lat, in_sem.at[3])
    lat_in.start()

    core, my_z = lax.rem(seg, 2), lax.rem(chan, SIDE)
    my_x = lax.rem(lax.div(seg, 2), SIDE)
    my_y = 2 * lax.div(chan, SIDE) + lax.div(seg, 2 * SIDE)
    steps = far_first()

    def coords(dz, dy, dx, dc):
        to_y = lax.rem(my_y + dy, SIDE)
        to_seg = 2 * SIDE * lax.rem(to_y, 2) + 2 * lax.rem(my_x + dx, SIDE) + lax.rem(core + dc, 2)
        return to_seg, SIDE * lax.div(to_y, 2) + lax.rem(my_z + dz, SIDE)

    barrier = pltpu.get_barrier_semaphore()
    for step in steps:
        pl.semaphore_signal(barrier, inc=1, device_id=coords(*step), device_id_type=MESH)

    def transform(h):
        step = half_rows
        low = lax.broadcasted_iota(jnp.int32, (step, 128), 0) % 8 < 4

        def block(i, carry):
            rows = pl.ds(pl.multiple_of(h * half_rows + i * step, step), step)
            y = lax.dot_general(tab[rows, :], sig[...], NT, preferred_element_type=jnp.float32)
            v = [y[:, q * 128 : (q + 1) * 128] for q in range(4)]
            up = [pltpu.roll(a, 4, 0) for a in v]
            even = [jnp.where(low, v[q], up[q + 1]) for q in (0, 2)]
            down = [pltpu.roll(a, step - 4, 0) for a in v]
            odd = [jnp.where(low, down[q], v[q + 1]) for q in (0, 2)]
            pairs = step // 8
            both = [
                jnp.concatenate([a.reshape(pairs, 1, 8, 128) for a in part], axis=2)
                for part in (even, odd)
            ]
            block = jnp.concatenate(both, axis=1).reshape(2 * pairs, 16, 128)
            send1[h, pl.ds(i * 2 * pairs, 2 * pairs)] = block.astype(jnp.bfloat16)
            return carry

        block(0, 0)

    def send(k, src, dst, at):
        for step in steps:
            to_seg, to_chan = coords(*step)
            pltpu.make_async_remote_copy(
                src_ref=src.at[to_seg * n_chan + to_chan], dst_ref=dst.at[at],
                send_sem=send_sem.at[k], recv_sem=recv_sem.at[k],
                device_id=(to_seg, to_chan), device_id_type=MESH,
            ).start()
        pltpu.make_async_copy(src.at[me], dst.at[at], recv_sem.at[k]).start()

    def arrived(k, src, dst):
        pltpu.make_async_copy(src, dst, recv_sem.at[k]).wait()

    def cross(h):
        width = n_seg * 16
        for j in range(n_chan):
            t = recv1[h, j * n_seg : (j + 1) * n_seg].reshape(width, 128).T
            for s in range(4):
                z[j * 32 : (j + 1) * 32, s * width : (s + 1) * width] = t[s * 32 : (s + 1) * 32]
        zf = z[...].astype(jnp.float32)
        lane = lax.broadcasted_iota(jnp.int32, zf.shape, 1) % 4
        last = zf.shape[1] - 1
        y = jnp.where(lane % 2 == 0, pltpu.roll(zf, last, 1), -pltpu.roll(zf, 1, 1))
        for b in range(2):
            own = lane // 2 == b
            for k, part in enumerate((zf, y)):
                right = jnp.where(own, part, 0.0).astype(jnp.bfloat16)
                c = lax.dot_general(z[...], right, NT, preferred_element_type=jnp.float32)
                for dh in range(2):
                    at = b * 4 + k * 2 + dh
                    scr[pl.ds(at, c.shape[0], stride=8), :] = c[:, dh * 128 : (dh + 1) * 128]
        send2[h] = scr[...].reshape(n, 16, 128).astype(jnp.bfloat16)

    def smooth(h):
        scr[...] = recv2[h].reshape(n * 16, 128).astype(jnp.float32)
        left = pl.ds(h * 2 * n, 2 * n)
        for c in range(2):
            for dh in range(2):
                for k in range(2):
                    at = c * 4 + dh * 2 + k
                    x = jnp.concatenate(
                        [
                            scr[pl.ds(c * 8 + b * 4 + k * 2 + dh, n, stride=16), :]
                            for b in range(2)
                        ],
                        axis=0,
                    ).astype(jnp.bfloat16)
                    r = jnp.dot(m_hi[:, left], x, preferred_element_type=jnp.float32)
                    r = r + jnp.dot(m_lo[:, left], x, preferred_element_type=jnp.float32)
                    if h == 0:
                        acc[at] = r
                    else:
                        out_ref[pl.ds(at, bins, stride=8), :] = r + acc[at]

    sig_in.wait()
    tab_in[0].wait()
    transform(0)
    pl.semaphore_wait(barrier, n - 1)
    send(0, send1.at[0], recv1.at[0], slot)
    tab_in[1].wait()
    transform(1)
    send(1, send1.at[1], recv1.at[1], slot)
    lat_in.wait()
    m = lax.dot_general(
        lat[...], lat[...], NT, preferred_element_type=jnp.float32, precision=lax.Precision.HIGHEST
    ) * (1.0 / segs)
    m_hi[...] = m.astype(jnp.bfloat16)
    m_lo[...] = (m - m_hi[...].astype(jnp.float32)).astype(jnp.bfloat16)
    for h in range(HALVES):
        arrived(h, send1.at[h], recv1.at[h])
        cross(h)
        send(2 + h, send2.at[h], recv2.at[h], me)
    for h in range(HALVES):
        arrived(2 + h, send2.at[h], recv2.at[h])
        smooth(h)
    for k in range(2 * HALVES):
        src = (send1, send2)[k // HALVES].at[k % HALVES, pl.ds(0, n - 1)]
        pltpu.make_async_copy(src, src, send_sem.at[k]).wait()


def per_device(signal, latent_factor):
    seg_count, chan_local, length = signal.shape
    bins, rank = latent_factor.shape
    n_seg = lax.axis_size("seg")
    n_chan = lax.axis_size("chan")
    n = n_seg * n_chan
    channels = chan_local * n_chan
    table = jnp.asarray(dft_rows(length, bins, n))
    bf16, f32 = jnp.bfloat16, jnp.float32
    out = pl.pallas_call(
        functools.partial(kernel, n_seg, n_chan, seg_count * n_seg),
        out_shape=jax.ShapeDtypeStruct((bins * 8, 128), f32),
        in_specs=[pl.BlockSpec(memory_space=pltpu.HBM)] * 3,
        out_specs=pl.BlockSpec(memory_space=pltpu.VMEM),
        scratch_shapes=[
            pltpu.VMEM((seg_count * chan_local, length), bf16),
            pltpu.VMEM(table.shape, bf16),
            pltpu.VMEM((bins, rank), f32),
            pltpu.VMEM((HALVES, n, 16, 128), bf16),
            pltpu.VMEM((HALVES, n, 16, 128), bf16),
            pltpu.VMEM((HALVES, n, 16, 128), bf16),
            pltpu.VMEM((HALVES, n, 16, 128), bf16),
            pltpu.VMEM((channels, 64 * n_seg), bf16),
            pltpu.VMEM((n * 16, 128), f32),
            pltpu.VMEM((bins, bins), bf16),
            pltpu.VMEM((bins, bins), bf16),
            pltpu.VMEM((8, bins, 128), f32),
            pltpu.SemaphoreType.DMA((4,)),
            pltpu.SemaphoreType.DMA((2 * HALVES,)),
            pltpu.SemaphoreType.DMA((2 * HALVES,)),
        ],
        compiler_params=pltpu.CompilerParams(
            collective_id=0, has_side_effects=True, vmem_limit_bytes=48 * 2**20
        ),
    )(pltpu.with_memory_space_constraint(signal.reshape(seg_count * chan_local, length), pltpu.HBM), table, pltpu.with_memory_space_constraint(latent_factor, pltpu.HBM))
    out = out.reshape(bins, 2, 2, 2, 128).transpose(0, 1, 3, 2, 4)
    return out.reshape(bins, channels // n, 2, channels)


def solution(mesh):
    in_specs = (P("seg", "chan", None), P())
    out_specs = P(None, ("seg", "chan"), None, None)
    return jax.shard_map(
        per_device, mesh=mesh, in_specs=in_specs, out_specs=out_specs, check_vma=False
    )
```

```python
import functools
import itertools
import random

import jax
import jax.numpy as jnp
import ml_dtypes
import numpy as np
from jax import lax
from jax.experimental import pallas as pl
from jax.experimental.pallas import tpu as pltpu
from jax.sharding import PartitionSpec as P

MESH = pl.DeviceIdType.MESH
HALVES = 2
SIDE = 4
NT = (((1,), (1,)), ((), ()))


def far_first():
    steps = [(z, y, x, c) for x in range(SIDE) for y in range(SIDE) for z in range(SIDE) for c in range(2)][1:]
    random.Random(1).shuffle(steps)
    return sorted(steps, key=lambda step: -sum(min(v, SIDE - v) for v in step[:3]))


def dft_rows(length, bins, devices):
    per_half = bins // devices // HALVES
    half, owner, at = np.meshgrid(
        np.arange(HALVES), np.arange(devices), np.arange(per_half), indexing="ij"
    )
    freqs = ((half * per_half + at) * devices + owner).reshape(-1)
    times = np.arange(length)
    theta = 2.0 * np.pi * (freqs[:, None] * times[None, :] % length) / length
    weight = (0.5 - 0.5 * np.cos(2.0 * np.pi * times / length)) / np.sqrt(3.0 * length / 8.0)
    rows = np.stack([weight * np.cos(theta), -weight * np.sin(theta)], axis=1)
    return rows.reshape(-1, length).astype(np.float32).astype(ml_dtypes.bfloat16)


def kernel(
    n_seg, n_chan, segs,
    sig_hbm, tab_hbm, lat_hbm, out_ref,
    sig, tab, lat, send1, recv1, send2, recv2, z, scr, m_hi, m_lo, acc,
    in_sem, send_sem, recv_sem,
):
    n = n_seg * n_chan
    seg, chan = lax.axis_index("seg"), lax.axis_index("chan")
    me = seg * n_chan + chan
    slot = chan * n_seg + seg
    half_rows = tab.shape[0] // HALVES
    bins = m_hi.shape[0]

    sig_in = pltpu.make_async_copy(sig_hbm, sig, in_sem.at[0])
    sig_in.start()
    tab_in = []
    for h in range(HALVES):
        rows = pl.ds(h * half_rows, half_rows)
        tab_in.append(pltpu.make_async_copy(tab_hbm.at[rows], tab.at[rows], in_sem.at[1 + h]))
    lat_in = pltpu.make_async_copy(lat_hbm, lat, in_sem.at[3])
    tab_in[0].start()

    core, my_z = lax.rem(seg, 2), lax.rem(chan, SIDE)
    my_x = lax.rem(lax.div(seg, 2), SIDE)
    my_y = 2 * lax.div(chan, SIDE) + lax.div(seg, 2 * SIDE)
    steps = far_first()

    def coords(dz, dy, dx, dc):
        to_y = lax.rem(my_y + dy, SIDE)
        to_seg = 2 * SIDE * lax.rem(to_y, 2) + 2 * lax.rem(my_x + dx, SIDE) + lax.rem(core + dc, 2)
        return to_seg, SIDE * lax.div(to_y, 2) + lax.rem(my_z + dz, SIDE)

    barrier = pltpu.get_barrier_semaphore()
    for step in itertools.product((2, 1, 3, 0), (2, 1, 3, 0), (2, 1, 3, 0), (1, 0)):
        if not any(step):
            continue
        pl.semaphore_signal(barrier, inc=1, device_id=coords(*step), device_id_type=MESH)
    tab_in[1].start()
    lat_in.start()

    def transform(h):
        low = lax.broadcasted_iota(jnp.int32, (half_rows, 128), 0) % 8 < 4
        rows = pl.ds(h * half_rows, half_rows)
        y = lax.dot_general(tab[rows, :], sig[...], NT, preferred_element_type=jnp.float32)
        v = [y[:, q * 128 : (q + 1) * 128] for q in range(4)]
        even = [jnp.where(low, v[q], pltpu.roll(v[q + 1], 4, 0)) for q in (0, 2)]
        odd = [jnp.where(low, pltpu.roll(v[q], half_rows - 4, 0), v[q + 1]) for q in (0, 2)]
        pairs = half_rows // 8
        both = [
            jnp.concatenate([a.reshape(pairs, 1, 8, 128) for a in part], axis=2)
            for part in (even, odd)
        ]
        send1[h] = jnp.concatenate(both, axis=1).reshape(n, 16, 128).astype(jnp.bfloat16)

    def send(k, src, dst, at):
        for step in steps:
            to_seg, to_chan = coords(*step)
            pltpu.make_async_remote_copy(
                src_ref=src.at[to_seg * n_chan + to_chan], dst_ref=dst.at[at],
                send_sem=send_sem.at[k], recv_sem=recv_sem.at[k],
                device_id=(to_seg, to_chan), device_id_type=MESH,
            ).start()
        pltpu.make_async_copy(src.at[me], dst.at[at], recv_sem.at[k]).start()

    def arrived(k, src, dst):
        pltpu.make_async_copy(src, dst, recv_sem.at[k]).wait()

    def cross(h):
        width = n_seg * 16
        for j in range(n_chan):
            t = recv1[h, j * n_seg : (j + 1) * n_seg].reshape(width, 128).T
            for s in range(4):
                z[j * 32 : (j + 1) * 32, s * width : (s + 1) * width] = t[s * 32 : (s + 1) * 32]
        zf = z[...].astype(jnp.float32)
        lane = lax.broadcasted_iota(jnp.int32, zf.shape, 1) % 4
        last = zf.shape[1] - 1
        y = jnp.where(lane % 2 == 0, pltpu.roll(zf, last, 1), -pltpu.roll(zf, 1, 1))
        for b in range(2):
            own = lane // 2 == b
            for k, part in enumerate((zf, y)):
                right = jnp.where(own, part, 0.0).astype(jnp.bfloat16)
                c = lax.dot_general(z[...], right, NT, preferred_element_type=jnp.float32)
                for dh in range(2):
                    at = b * 4 + k * 2 + dh
                    scr[pl.ds(at, c.shape[0], stride=8), :] = c[:, dh * 128 : (dh + 1) * 128]
        send2[h] = scr[...].reshape(n, 16, 128).astype(jnp.bfloat16)

    def smooth(h):
        scr[...] = recv2[h].reshape(n * 16, 128).astype(jnp.float32)
        left = pl.ds(h * 2 * n, 2 * n)
        for c in range(2):
            for dh in range(2):
                cols = [
                    jnp.concatenate(
                        [
                            scr[pl.ds(c * 8 + b * 4 + k * 2 + dh, n, stride=16), :]
                            for b in range(2)
                        ],
                        axis=0,
                    ).astype(jnp.bfloat16)
                    for k in range(2)
                ]
                x = jnp.concatenate(cols, axis=1)
                r = jnp.dot(m_hi[:, left], x, preferred_element_type=jnp.float32)
                r = r + jnp.dot(m_lo[:, left], x, preferred_element_type=jnp.float32)
                for k in range(2):
                    at = c * 4 + dh * 2 + k
                    part = r[:, k * 128 : (k + 1) * 128]
                    if h == 0:
                        acc[at] = part
                    else:
                        out_ref[pl.ds(at, bins, stride=8), :] = part + acc[at]

    sig_in.wait()
    tab_in[0].wait()
    transform(0)
    pl.semaphore_wait(barrier, n - 1)
    send(0, send1.at[0], recv1.at[0], slot)
    tab_in[1].wait()
    transform(1)
    send(1, send1.at[1], recv1.at[1], slot)
    lat_in.wait()
    m = lax.dot_general(
        lat[...], lat[...], NT, preferred_element_type=jnp.float32, precision=lax.Precision.HIGHEST
    ) * (1.0 / segs)
    m_hi[...] = m.astype(jnp.bfloat16)
    m_lo[...] = (m - m_hi[...].astype(jnp.float32)).astype(jnp.bfloat16)
    for h in range(HALVES):
        arrived(h, send1.at[h], recv1.at[h])
        cross(h)
        send(2 + h, send2.at[h], recv2.at[h], me)
    for h in range(HALVES):
        arrived(2 + h, send2.at[h], recv2.at[h])
        smooth(h)
    for k in range(2 * HALVES):
        src = (send1, send2)[k // HALVES].at[k % HALVES, pl.ds(0, n - 1)]
        pltpu.make_async_copy(src, src, send_sem.at[k]).wait()


def per_device(signal, latent_factor):
    seg_count, chan_local, length = signal.shape
    bins, rank = latent_factor.shape
    n_seg = lax.axis_size("seg")
    n_chan = lax.axis_size("chan")
    n = n_seg * n_chan
    channels = chan_local * n_chan
    table = jnp.asarray(dft_rows(length, bins, n))
    bf16, f32 = jnp.bfloat16, jnp.float32
    out = pl.pallas_call(
        functools.partial(kernel, n_seg, n_chan, seg_count * n_seg),
        out_shape=jax.ShapeDtypeStruct((bins * 8, 128), f32),
        in_specs=[pl.BlockSpec(memory_space=pltpu.HBM)] * 3,
        out_specs=pl.BlockSpec(memory_space=pltpu.VMEM),
        scratch_shapes=[
            pltpu.VMEM((seg_count * chan_local, length), bf16),
            pltpu.VMEM(table.shape, bf16),
            pltpu.VMEM((bins, rank), f32),
            pltpu.VMEM((HALVES, n, 16, 128), bf16),
            pltpu.VMEM((HALVES, n, 16, 128), bf16),
            pltpu.VMEM((HALVES, n, 16, 128), bf16),
            pltpu.VMEM((HALVES, n, 16, 128), bf16),
            pltpu.VMEM((channels, 64 * n_seg), bf16),
            pltpu.VMEM((n * 16, 128), f32),
            pltpu.VMEM((bins, bins), bf16),
            pltpu.VMEM((bins, bins), bf16),
            pltpu.VMEM((8, bins, 128), f32),
            pltpu.SemaphoreType.DMA((4,)),
            pltpu.SemaphoreType.DMA((2 * HALVES,)),
            pltpu.SemaphoreType.DMA((2 * HALVES,)),
        ],
        compiler_params=pltpu.CompilerParams(
            collective_id=0, has_side_effects=True, vmem_limit_bytes=48 * 2**20
        ),
    )(pltpu.with_memory_space_constraint(signal.reshape(seg_count * chan_local, length), pltpu.HBM), table, pltpu.with_memory_space_constraint(latent_factor, pltpu.HBM))
    out = out.reshape(bins, 2, 2, 2, 128).transpose(0, 1, 3, 2, 4)
    return out.reshape(bins, channels // n, 2, channels)


def solution(mesh):
    in_specs = (P("seg", "chan", None), P())
    out_specs = P(None, ("seg", "chan"), None, None)
    return jax.shard_map(
        per_device, mesh=mesh, in_specs=in_specs, out_specs=out_specs, check_vma=False
    )
```

```python
import functools
import itertools
import random

import jax
import jax.numpy as jnp
import ml_dtypes
import numpy as np
from jax import lax
from jax.experimental import pallas as pl
from jax.experimental.pallas import tpu as pltpu
from jax.sharding import PartitionSpec as P

MESH = pl.DeviceIdType.MESH
HALVES = 2
SIDE = 4
NT = (((1,), (1,)), ((), ()))


def far_first():
    steps = [(z, y, x, c) for x in range(SIDE) for y in range(SIDE) for z in range(SIDE) for c in range(2)][1:]
    random.Random(1).shuffle(steps)
    return sorted(steps, key=lambda step: -sum(min(v, SIDE - v) for v in step[:3]))


def dft_rows(length, bins, devices):
    per_half = bins // devices // HALVES
    half, owner, at = np.meshgrid(
        np.arange(HALVES), np.arange(devices), np.arange(per_half), indexing="ij"
    )
    freqs = ((half * per_half + at) * devices + owner).reshape(-1)
    times = np.arange(length)
    theta = 2.0 * np.pi * (freqs[:, None] * times[None, :] % length) / length
    weight = (0.5 - 0.5 * np.cos(2.0 * np.pi * times / length)) / np.sqrt(3.0 * length / 8.0)
    rows = np.stack([weight * np.cos(theta), -weight * np.sin(theta)], axis=1)
    return rows.reshape(-1, length).astype(np.float32).astype(ml_dtypes.bfloat16)


def kernel(
    n_seg, n_chan, segs,
    sig_hbm, tab_hbm, lat_hbm, out_ref,
    sig, tab, lat, send1, recv1, send2, recv2, z, scr, m_hi, m_lo, acc,
    in_sem, send_sem, recv_sem,
):
    n = n_seg * n_chan
    seg, chan = lax.axis_index("seg"), lax.axis_index("chan")
    me = seg * n_chan + chan
    slot = chan * n_seg + seg
    half_rows = tab.shape[0] // HALVES
    bins = m_hi.shape[0]

    sig_in = pltpu.make_async_copy(sig_hbm, sig, in_sem.at[0])
    sig_in.start()
    tab_in = []
    for h in range(HALVES):
        rows = pl.ds(h * half_rows, half_rows)
        tab_in.append(pltpu.make_async_copy(tab_hbm.at[rows], tab.at[rows], in_sem.at[1 + h]))
    lat_in = pltpu.make_async_copy(lat_hbm, lat, in_sem.at[3])
    tab_in[0].start()

    core, my_z = lax.rem(seg, 2), lax.rem(chan, SIDE)
    my_x = lax.rem(lax.div(seg, 2), SIDE)
    my_y = 2 * lax.div(chan, SIDE) + lax.div(seg, 2 * SIDE)
    steps = far_first()

    def coords(dz, dy, dx, dc):
        to_y = lax.rem(my_y + dy, SIDE)
        to_seg = 2 * SIDE * lax.rem(to_y, 2) + 2 * lax.rem(my_x + dx, SIDE) + lax.rem(core + dc, 2)
        return to_seg, SIDE * lax.div(to_y, 2) + lax.rem(my_z + dz, SIDE)

    barrier = pltpu.get_barrier_semaphore()
    for step in itertools.product((2, 1, 3, 0), (2, 1, 3, 0), (2, 1, 3, 0), (1, 0)):
        if not any(step):
            continue
        pl.semaphore_signal(barrier, inc=1, device_id=coords(*step), device_id_type=MESH)
    tab_in[1].start()
    lat_in.start()

    def transform(h):
        low = lax.broadcasted_iota(jnp.int32, (half_rows, 128), 0) % 8 < 4
        rows = pl.ds(h * half_rows, half_rows)
        y = lax.dot_general(tab[rows, :], sig[...], NT, preferred_element_type=jnp.float32)
        v = [y[:, q * 128 : (q + 1) * 128] for q in range(4)]
        even = [jnp.where(low, v[q], pltpu.roll(v[q + 1], 4, 0)) for q in (0, 2)]
        odd = [jnp.where(low, pltpu.roll(v[q], half_rows - 4, 0), v[q + 1]) for q in (0, 2)]
        pairs = half_rows // 8
        both = [
            jnp.concatenate([a.reshape(pairs, 1, 8, 128) for a in part], axis=2)
            for part in (even, odd)
        ]
        send1[h] = jnp.concatenate(both, axis=1).reshape(n, 16, 128).astype(jnp.bfloat16)

    def send(k, src, dst, at):
        for step in steps:
            to_seg, to_chan = coords(*step)
            pltpu.make_async_remote_copy(
                src_ref=src.at[to_seg * n_chan + to_chan], dst_ref=dst.at[at],
                send_sem=send_sem.at[k], recv_sem=recv_sem.at[k],
                device_id=(to_seg, to_chan), device_id_type=MESH,
            ).start()
        pltpu.make_async_copy(src.at[me], dst.at[at], recv_sem.at[k]).start()

    def arrived(k, src, dst):
        pltpu.make_async_copy(src, dst, recv_sem.at[k]).wait()

    def cross(h):
        width = n_seg * 16
        for j in range(n_chan):
            t = recv1[h, j * n_seg : (j + 1) * n_seg].reshape(width, 128).T
            for s in range(4):
                z[j * 32 : (j + 1) * 32, s * width : (s + 1) * width] = t[s * 32 : (s + 1) * 32]
        zf = z[...].astype(jnp.float32)
        lane = lax.broadcasted_iota(jnp.int32, zf.shape, 1) % 4
        last = zf.shape[1] - 1
        y = jnp.where(lane % 2 == 0, pltpu.roll(zf, last, 1), -pltpu.roll(zf, 1, 1))
        for b in range(2):
            own = lane // 2 == b
            for k, part in enumerate((zf, y)):
                right = jnp.where(own, part, 0.0).astype(jnp.bfloat16)
                c = lax.dot_general(z[...], right, NT, preferred_element_type=jnp.float32)
                for dh in range(2):
                    at = b * 4 + k * 2 + dh
                    scr[pl.ds(at, c.shape[0], stride=8), :] = c[:, dh * 128 : (dh + 1) * 128]
        send2[h] = scr[...].reshape(n, 16, 128).astype(jnp.bfloat16)

    def smooth(h):
        scr[...] = recv2[h].reshape(n * 16, 128).astype(jnp.float32)
        left = pl.ds(h * 2 * n, 2 * n)
        for c in range(2):
            for dh in range(2):
                cols = [
                    jnp.concatenate(
                        [
                            scr[pl.ds(c * 8 + b * 4 + k * 2 + dh, n, stride=16), :]
                            for b in range(2)
                        ],
                        axis=0,
                    ).astype(jnp.bfloat16)
                    for k in range(2)
                ]
                x = jnp.concatenate(cols, axis=1)
                r = jnp.dot(m_hi[:, left], x, preferred_element_type=jnp.float32)
                r = r + jnp.dot(m_lo[:, left], x, preferred_element_type=jnp.float32)
                for k in range(2):
                    at = c * 4 + dh * 2 + k
                    part = r[:, k * 128 : (k + 1) * 128]
                    if h == 0:
                        acc[at] = part
                    else:
                        out_ref[pl.ds(at, bins, stride=8), :] = part + acc[at]

    sig_in.wait()
    tab_in[0].wait()
    transform(0)
    pl.semaphore_wait(barrier, n - 1)
    send(0, send1.at[0], recv1.at[0], slot)
    tab_in[1].wait()
    transform(1)
    send(1, send1.at[1], recv1.at[1], slot)
    lat_in.wait()
    m = lax.dot_general(
        lat[...], lat[...], NT, preferred_element_type=jnp.float32, precision=lax.Precision.HIGHEST
    ) * (1.0 / segs)
    m_hi[...] = m.astype(jnp.bfloat16)
    m_lo[...] = (m - m_hi[...].astype(jnp.float32)).astype(jnp.bfloat16)
    for h in range(HALVES):
        arrived(h, send1.at[h], recv1.at[h])
        cross(h)
        send(2 + h, send2.at[h], recv2.at[h], me)
    def sent(k):
        src = (send1, send2)[k // HALVES].at[k % HALVES, pl.ds(0, n - 1)]
        pltpu.make_async_copy(src, src, send_sem.at[k]).wait()

    for h in range(HALVES):
        if h == HALVES - 1:
            for k in range(2 * HALVES):
                sent(k)
        arrived(2 + h, send2.at[h], recv2.at[h])
        smooth(h)


def per_device(signal, latent_factor):
    seg_count, chan_local, length = signal.shape
    bins, rank = latent_factor.shape
    n_seg = lax.axis_size("seg")
    n_chan = lax.axis_size("chan")
    n = n_seg * n_chan
    channels = chan_local * n_chan
    table = jnp.asarray(dft_rows(length, bins, n))
    bf16, f32 = jnp.bfloat16, jnp.float32
    out = pl.pallas_call(
        functools.partial(kernel, n_seg, n_chan, seg_count * n_seg),
        out_shape=jax.ShapeDtypeStruct((bins * 8, 128), f32),
        in_specs=[pl.BlockSpec(memory_space=pltpu.HBM)] * 3,
        out_specs=pl.BlockSpec(memory_space=pltpu.VMEM),
        scratch_shapes=[
            pltpu.VMEM((seg_count * chan_local, length), bf16),
            pltpu.VMEM(table.shape, bf16),
            pltpu.VMEM((bins, rank), f32),
            pltpu.VMEM((HALVES, n, 16, 128), bf16),
            pltpu.VMEM((HALVES, n, 16, 128), bf16),
            pltpu.VMEM((HALVES, n, 16, 128), bf16),
            pltpu.VMEM((HALVES, n, 16, 128), bf16),
            pltpu.VMEM((channels, 64 * n_seg), bf16),
            pltpu.VMEM((n * 16, 128), f32),
            pltpu.VMEM((bins, bins), bf16),
            pltpu.VMEM((bins, bins), bf16),
            pltpu.VMEM((8, bins, 128), f32),
            pltpu.SemaphoreType.DMA((4,)),
            pltpu.SemaphoreType.DMA((2 * HALVES,)),
            pltpu.SemaphoreType.DMA((2 * HALVES,)),
        ],
        compiler_params=pltpu.CompilerParams(
            collective_id=0, has_side_effects=True, vmem_limit_bytes=48 * 2**20
        ),
    )(pltpu.with_memory_space_constraint(signal.reshape(seg_count * chan_local, length), pltpu.HBM), table, pltpu.with_memory_space_constraint(latent_factor, pltpu.HBM))
    out = out.reshape(bins, 2, 2, 2, 128).transpose(0, 1, 3, 2, 4)
    return out.reshape(bins, channels // n, 2, channels)


def solution(mesh):
    in_specs = (P("seg", "chan", None), P())
    out_specs = P(None, ("seg", "chan"), None, None)
    return jax.shard_map(
        per_device, mesh=mesh, in_specs=in_specs, out_specs=out_specs, check_vma=False
    )
```

```python
import functools
import itertools
import random

import jax
import jax.numpy as jnp
import ml_dtypes
import numpy as np
from jax import lax
from jax.experimental import pallas as pl
from jax.experimental.pallas import tpu as pltpu
from jax.sharding import PartitionSpec as P

MESH = pl.DeviceIdType.MESH
HALVES = 2
SIDE = 4
NT = (((1,), (1,)), ((), ()))


def far_first():
    steps = [(z, y, x, c) for x in range(SIDE) for y in range(SIDE) for z in range(SIDE) for c in range(2)][1:]
    random.Random(1).shuffle(steps)
    return sorted(steps, key=lambda step: -sum(min(v, SIDE - v) for v in step[:3]))


def dft_rows(length, bins, devices):
    per_half = bins // devices // HALVES
    half, owner, at = np.meshgrid(
        np.arange(HALVES), np.arange(devices), np.arange(per_half), indexing="ij"
    )
    freqs = ((half * per_half + at) * devices + owner).reshape(-1)
    times = np.arange(length)
    theta = 2.0 * np.pi * (freqs[:, None] * times[None, :] % length) / length
    weight = (0.5 - 0.5 * np.cos(2.0 * np.pi * times / length)) / np.sqrt(3.0 * length / 8.0)
    rows = np.stack([weight * np.cos(theta), -weight * np.sin(theta)], axis=1)
    return rows.reshape(-1, length).astype(np.float32).astype(ml_dtypes.bfloat16)


def kernel(
    n_seg, n_chan, segs,
    sig_hbm, tab_hbm, lat_hbm, out_ref,
    sig, tab, lat, send1, recv1, send2, recv2, z, scr, m_hi, m_lo, acc,
    in_sem, send_sem, recv_sem,
):
    n = n_seg * n_chan
    seg, chan = lax.axis_index("seg"), lax.axis_index("chan")
    me = seg * n_chan + chan
    slot = chan * n_seg + seg
    half_rows = tab.shape[0] // HALVES
    bins = m_hi.shape[0]

    sig_in = pltpu.make_async_copy(sig_hbm, sig, in_sem.at[0])
    sig_in.start()
    tab_in = []
    for h in range(HALVES):
        rows = pl.ds(h * half_rows, half_rows)
        tab_in.append(pltpu.make_async_copy(tab_hbm.at[rows], tab.at[rows], in_sem.at[1 + h]))
    lat_in = pltpu.make_async_copy(lat_hbm, lat, in_sem.at[3])
    tab_in[0].start()

    core, my_z = lax.rem(seg, 2), lax.rem(chan, SIDE)
    my_x = lax.rem(lax.div(seg, 2), SIDE)
    my_y = 2 * lax.div(chan, SIDE) + lax.div(seg, 2 * SIDE)
    steps = far_first()

    def coords(dz, dy, dx, dc):
        to_y = lax.rem(my_y + dy, SIDE)
        to_seg = 2 * SIDE * lax.rem(to_y, 2) + 2 * lax.rem(my_x + dx, SIDE) + lax.rem(core + dc, 2)
        return to_seg, SIDE * lax.div(to_y, 2) + lax.rem(my_z + dz, SIDE)

    barrier = pltpu.get_barrier_semaphore()
    for step in itertools.product((2, 1, 3, 0), (2, 1, 3, 0), (2, 1, 3, 0), (1, 0)):
        if not any(step):
            continue
        pl.semaphore_signal(barrier, inc=1, device_id=coords(*step), device_id_type=MESH)
    tab_in[1].start()
    lat_in.start()

    def transform(h):
        low = lax.broadcasted_iota(jnp.int32, (half_rows, 128), 0) % 8 < 4
        rows = pl.ds(h * half_rows, half_rows)
        y = lax.dot_general(tab[rows, :], sig[...], NT, preferred_element_type=jnp.float32)
        v = [y[:, q * 128 : (q + 1) * 128] for q in range(4)]
        even = [jnp.where(low, v[q], pltpu.roll(v[q + 1], 4, 0)) for q in (0, 2)]
        odd = [jnp.where(low, pltpu.roll(v[q], half_rows - 4, 0), v[q + 1]) for q in (0, 2)]
        pairs = half_rows // 8
        both = [
            jnp.concatenate([a.reshape(pairs, 1, 8, 128) for a in part], axis=2)
            for part in (even, odd)
        ]
        send1[h] = jnp.concatenate(both, axis=1).reshape(n, 16, 128).astype(jnp.bfloat16)

    def send(k, src, dst, at):
        pltpu.make_async_copy(src.at[me], dst.at[at], recv_sem.at[k]).start()
        for step in steps:
            to_seg, to_chan = coords(*step)
            pltpu.make_async_remote_copy(
                src_ref=src.at[to_seg * n_chan + to_chan], dst_ref=dst.at[at],
                send_sem=send_sem.at[k], recv_sem=recv_sem.at[k],
                device_id=(to_seg, to_chan), device_id_type=MESH,
            ).start()

    def arrived(k, src, dst):
        pltpu.make_async_copy(src, dst, recv_sem.at[k]).wait()

    def cross(h):
        width = n_seg * 16
        for j in range(n_chan):
            t = recv1[h, j * n_seg : (j + 1) * n_seg].reshape(width, 128).T
            for s in range(4):
                z[j * 32 : (j + 1) * 32, s * width : (s + 1) * width] = t[s * 32 : (s + 1) * 32]
        zf = z[...].astype(jnp.float32)
        lane = lax.broadcasted_iota(jnp.int32, zf.shape, 1) % 4
        last = zf.shape[1] - 1
        y = jnp.where(lane % 2 == 0, pltpu.roll(zf, last, 1), -pltpu.roll(zf, 1, 1))
        for b in range(2):
            own = lane // 2 == b
            for k, part in enumerate((zf, y)):
                right = jnp.where(own, part, 0.0).astype(jnp.bfloat16)
                c = lax.dot_general(z[...], right, NT, preferred_element_type=jnp.float32)
                for dh in range(2):
                    at = b * 4 + k * 2 + dh
                    scr[pl.ds(at, c.shape[0], stride=8), :] = c[:, dh * 128 : (dh + 1) * 128]
        send2[h] = scr[...].reshape(n, 16, 128).astype(jnp.bfloat16)

    def smooth(h):
        scr[...] = recv2[h].reshape(n * 16, 128).astype(jnp.float32)
        left = pl.ds(h * 2 * n, 2 * n)
        for c in range(2):
            for dh in range(2):
                cols = [
                    jnp.concatenate(
                        [
                            scr[pl.ds(c * 8 + b * 4 + k * 2 + dh, n, stride=16), :]
                            for b in range(2)
                        ],
                        axis=0,
                    ).astype(jnp.bfloat16)
                    for k in range(2)
                ]
                x = jnp.concatenate(cols, axis=1)
                r = jnp.dot(m_hi[:, left], x, preferred_element_type=jnp.float32)
                r = r + jnp.dot(m_lo[:, left], x, preferred_element_type=jnp.float32)
                for k in range(2):
                    at = c * 4 + dh * 2 + k
                    part = r[:, k * 128 : (k + 1) * 128]
                    if h == 0:
                        acc[at] = part
                    else:
                        out_ref[pl.ds(at, bins, stride=8), :] = part + acc[at]

    sig_in.wait()
    tab_in[0].wait()
    transform(0)
    pl.semaphore_wait(barrier, n - 1)
    send(0, send1.at[0], recv1.at[0], slot)
    tab_in[1].wait()
    transform(1)
    send(1, send1.at[1], recv1.at[1], slot)
    lat_in.wait()
    m = lax.dot_general(
        lat[...], lat[...], NT, preferred_element_type=jnp.float32, precision=lax.Precision.HIGHEST
    ) * (1.0 / segs)
    m_hi[...] = m.astype(jnp.bfloat16)
    m_lo[...] = (m - m_hi[...].astype(jnp.float32)).astype(jnp.bfloat16)
    for h in range(HALVES):
        arrived(h, send1.at[h], recv1.at[h])
        cross(h)
        send(2 + h, send2.at[h], recv2.at[h], me)
    def sent(k):
        src = (send1, send2)[k // HALVES].at[k % HALVES, pl.ds(0, n - 1)]
        pltpu.make_async_copy(src, src, send_sem.at[k]).wait()

    for h in range(HALVES):
        if h == HALVES - 1:
            for k in range(2 * HALVES):
                sent(k)
        arrived(2 + h, send2.at[h], recv2.at[h])
        smooth(h)


def per_device(signal, latent_factor):
    seg_count, chan_local, length = signal.shape
    bins, rank = latent_factor.shape
    n_seg = lax.axis_size("seg")
    n_chan = lax.axis_size("chan")
    n = n_seg * n_chan
    channels = chan_local * n_chan
    table = jnp.asarray(dft_rows(length, bins, n))
    bf16, f32 = jnp.bfloat16, jnp.float32
    out = pl.pallas_call(
        functools.partial(kernel, n_seg, n_chan, seg_count * n_seg),
        out_shape=jax.ShapeDtypeStruct((bins * 8, 128), f32),
        in_specs=[pl.BlockSpec(memory_space=pltpu.HBM)] * 3,
        out_specs=pl.BlockSpec(memory_space=pltpu.VMEM),
        scratch_shapes=[
            pltpu.VMEM((seg_count * chan_local, length), bf16),
            pltpu.VMEM(table.shape, bf16),
            pltpu.VMEM((bins, rank), f32),
            pltpu.VMEM((HALVES, n, 16, 128), bf16),
            pltpu.VMEM((HALVES, n, 16, 128), bf16),
            pltpu.VMEM((HALVES, n, 16, 128), bf16),
            pltpu.VMEM((HALVES, n, 16, 128), bf16),
            pltpu.VMEM((channels, 64 * n_seg), bf16),
            pltpu.VMEM((n * 16, 128), f32),
            pltpu.VMEM((bins, bins), bf16),
            pltpu.VMEM((bins, bins), bf16),
            pltpu.VMEM((8, bins, 128), f32),
            pltpu.SemaphoreType.DMA((4,)),
            pltpu.SemaphoreType.DMA((2 * HALVES,)),
            pltpu.SemaphoreType.DMA((2 * HALVES,)),
        ],
        compiler_params=pltpu.CompilerParams(
            collective_id=0, has_side_effects=True, vmem_limit_bytes=48 * 2**20
        ),
    )(pltpu.with_memory_space_constraint(signal.reshape(seg_count * chan_local, length), pltpu.HBM), table, pltpu.with_memory_space_constraint(latent_factor, pltpu.HBM))
    out = out.reshape(bins, 2, 2, 2, 128).transpose(0, 1, 3, 2, 4)
    return out.reshape(bins, channels // n, 2, channels)


def solution(mesh):
    in_specs = (P("seg", "chan", None), P())
    out_specs = P(None, ("seg", "chan"), None, None)
    return jax.shard_map(
        per_device, mesh=mesh, in_specs=in_specs, out_specs=out_specs, check_vma=False
    )
```
